128 devices in a mesh: gossip: 8 (over z, y_lo), tp: 16 (over y_hi, x, core).
Axes of the slice: x: 4, y: 4 (y_hi: 2, y_lo: 2; y = y_hi * 2 + y_lo), z: 4, core: 2. Of those that a mesh axis runs over, the one named last changes fastest.
Arguments:
- tokens: bfloat16 [8, 1024, 5120], P('gossip', 'tp'), may hold values from -6 to 6
- token_ids: int32 [8, 1024], P('gossip'), may hold values from 0 to 151935, as said below
- cotangent: bfloat16 [8, 1024, 5120], P('gossip', 'tp'), may hold values from -48 to 48
- step_index: int32 [1], replicated, may hold values from 0 to 999
- norm_gain: float32 [5120], replicated, may hold values from 0.1 to 1.9
- q_gain: float32 [128], replicated, may hold values from 0.1 to 1.9
- k_gain: float32 [128], replicated, may hold values from 0.1 to 1.9
- w_query: bfloat16 [8, 5120, 4096], P('gossip', None, 'tp'), may hold values from -6 to 6
- w_keyval: bfloat16 [8, 1024, 5120], P('gossip', 'tp'), may hold values from -6 to 6
- w_out: bfloat16 [8, 4096, 5120], P('gossip', 'tp'), may hold values from -6 to 6
- m_query: bfloat16 [8, 5120, 4096], P('gossip', None, 'tp'), may hold values from -6 to 6
- m_keyval: bfloat16 [8, 1024, 5120], P('gossip', 'tp'), may hold values from -6 to 6
- m_out: bfloat16 [8, 4096, 5120], P('gossip', 'tp'), may hold values from -6 to 6
Outputs:
- attended: bfloat16 [8, 1024, 5120], P('gossip', 'tp')
- avg_query: bfloat16 [8, 5120, 4096], P('gossip', None, 'tp')
- avg_keyval: bfloat16 [8, 1024, 5120], P('gossip', 'tp')
- avg_out: bfloat16 [8, 4096, 5120], P('gossip', 'tp')
- new_m_query: bfloat16 [8, 5120, 4096], P('gossip', None, 'tp')
- new_m_keyval: bfloat16 [8, 1024, 5120], P('gossip', 'tp')
- new_m_out: bfloat16 [8, 4096, 5120], P('gossip', 'tp')
The draws below stay inside these ranges and needn't reach their ends.
Inputs may be any that keep to these rules, and one draw needn't show every extreme that they name: `token_ids`: ids of a group's tokens; id 151643 ends a document.
All inputs are finite; a program needn't handle non-finite values.
Results may differ from the reference program's by a relative error of at most 0.019.
Values may be sent and summed in bfloat16 or wider, within the bound.
No kernel may reach another device: no remote copies, remote signals or barrier semaphores. Data moves between devices by JAX's collectives and lax.ppermute only.
A program may use at most 192 MiB of HBM per device.

```python
import math
import jax
import jax.numpy as jnp
from jax import lax

D = 5120
HD = 128
QH = 32
KVH = 4
S = 1024
GROUPS = 8
N_GOSSIP = 8
N_TP = 16


def draw_token_ids(key, part):
    key = jax.random.fold_in(key, 11)
    pick_key, end_key = jax.random.split(key)
    drawn = jax.random.randint(pick_key, (GROUPS, S), 0, 151936, dtype=jnp.int32)
    closing = jax.random.randint(end_key, (GROUPS, S), 0, 48, dtype=jnp.int32) == 0
    return jnp.where(closing, jnp.int32(151643), drawn).astype(jnp.int32)


def block_scale(rng, extent, pieces, low, top_value):
    level = 1.0
    for dim, shards_of in pieces:
        draws = jax.random.uniform(jax.random.fold_in(jax.random.fold_in(rng, 6), dim), (shards_of,), jnp.float32, low / len(pieces), top_value / len(pieces))
        level = level * jnp.repeat(jnp.exp(draws), extent[dim] // shards_of).reshape((-1,) + (1,) * (len(extent) - 1 - dim))
    return level


def noise(rng, dims, spread, limit, cuts=(), held_as=jnp.bfloat16):
    values = spread * jax.random.normal(rng, dims, jnp.float32)
    if cuts:
        values = values * block_scale(rng, dims, cuts, -0.22, 0.18)
    return jnp.clip(values, -limit, limit).astype(held_as)


def setup_inputs(seed: int = 0) -> dict:
    key_list = jax.random.split(jax.random.key(seed), 14)
    return {
        "tokens": noise(key_list[0], (GROUPS, S, D), 1.0, 6.0, ((0, 8), (1, 16))),
        "token_ids": draw_token_ids(jax.random.fold_in(key_list[13], 71), 0),
        "cotangent": noise(key_list[2], (GROUPS, S, D), 8.0, 48.0, ((0, 8), (1, 16))),
        "step_index": jax.random.randint(key_list[3], (1,), 0, 1000).astype(jnp.int32),
        "norm_gain": jnp.clip(1.0 + 0.18 * jax.random.normal(key_list[4], (D,), jnp.float32), 0.1, 1.9),
        "q_gain": jnp.clip(1.0 + 0.18 * jax.random.normal(key_list[5], (HD,), jnp.float32), 0.1, 1.9),
        "k_gain": jnp.clip(1.0 + 0.18 * jax.random.normal(key_list[6], (HD,), jnp.float32), 0.1, 1.9),
        "w_query": noise(key_list[7], (GROUPS, D, QH * HD), 1.0, 6.0, ((0, 8), (2, 16))),
        "w_keyval": noise(key_list[8], (GROUPS, 2 * KVH * HD, D), 1.0, 6.0, ((0, 8), (1, 16))),
        "w_out": noise(key_list[9], (GROUPS, QH * HD, D), 1.0, 6.0, ((0, 8), (1, 16))),
        "m_query": noise(key_list[10], (GROUPS, D, QH * HD), 1.0, 6.0, ((0, 8), (2, 16))),
        "m_keyval": noise(key_list[11], (GROUPS, 2 * KVH * HD, D), 1.0, 6.0, ((0, 8), (1, 16))),
        "m_out": noise(key_list[12], (GROUPS, QH * HD, D), 1.0, 6.0, ((0, 8), (1, 16))),
    }


norm_eps = 1e-06
rope_base = 1000000.0
end_token = 151643
peak_rate = 0.2
momentum_keep = 0.9

def warm_rate(step_index):
    return peak_rate * (step_index[0] + 1).astype(jnp.float32) / 1000.0

def normalize(token_rows, gain):
    floats = token_rows.astype(jnp.float32)
    scale = lax.rsqrt(lax.optimization_barrier(jnp.mean(floats * floats, axis=-1, keepdims=True)) + norm_eps)
    return (floats * scale * gain).astype(jnp.bfloat16)

def rotary_tables(length, head_width):
    positions = jnp.arange(length, dtype=jnp.float32)[:, None]
    inverse_freq = rope_base ** (-2.0 * jnp.arange(head_width // 2, dtype=jnp.float32) / head_width)
    angles = positions * inverse_freq
    return (jnp.cos(angles), jnp.sin(angles))

def rotate(values, cosine, sine):
    half_width = values.shape[-1] // 2
    first_half = values[..., :half_width]
    second_half = values[..., half_width:]
    return jnp.concatenate([first_half * cosine - second_half * sine, second_half * cosine + first_half * sine], axis=-1)

def allowed_pairs(token_ids):
    closing = (token_ids == end_token).astype(jnp.int32)
    document = jnp.cumsum(closing) - closing
    places = jnp.arange(token_ids.shape[0], dtype=jnp.int32)
    return (places[None, :] <= places[:, None]) & (document[None, :] == document[:, None])

def heads_forward(query_raw, key_raw, values, q_gain, k_gain, cosine, sine, allowed):
    length = query_raw.shape[0]
    head_width = key_raw.shape[1]
    query = query_raw.reshape(length, -1, head_width)
    query_norm = query * lax.rsqrt(lax.optimization_barrier(jnp.mean(query * query, axis=-1, keepdims=True)) + norm_eps) * q_gain
    query_rot = rotate(query_norm, cosine[:, None, :], sine[:, None, :]).astype(jnp.bfloat16)
    key_float = key_raw.astype(jnp.float32)
    key_norm = key_float * lax.rsqrt(lax.optimization_barrier(jnp.mean(key_float * key_float, axis=-1, keepdims=True)) + norm_eps) * k_gain
    key_rot = rotate(key_norm, cosine, sine).astype(jnp.bfloat16)
    scores = jnp.einsum('snd,td->nst', query_rot.astype(jnp.float32), key_rot.astype(jnp.float32)) / math.sqrt(head_width)
    weights = jnp.where(allowed[None, :, :], jnp.exp(scores), 0.0)
    probabilities = (weights / lax.optimization_barrier(jnp.sum(weights, axis=-1, keepdims=True))).astype(jnp.bfloat16)
    head_mix = jnp.einsum('nst,td->snd', probabilities.astype(jnp.float32), values.astype(jnp.float32))
    return head_mix.reshape(length, -1).astype(jnp.bfloat16)

def advance(weight, moment, gradient, step_rate):
    new_moment = momentum_keep * moment.astype(jnp.float32) + gradient
    stepped = (weight.astype(jnp.float32) - step_rate * new_moment).astype(jnp.bfloat16)
    return (stepped, new_moment.astype(jnp.bfloat16))

def group_window(token_rows, token_ids, cotangent, w_query, w_keyval, w_out, m_query, m_keyval, m_out, norm_gain, q_gain, k_gain, step_rate):
    length = token_rows.shape[0]
    root_d = math.sqrt(D)
    root_q = math.sqrt(QH * HD)
    normed = normalize(token_rows, norm_gain)
    keyval = (jnp.dot(normed, w_keyval.T, preferred_element_type=jnp.float32) / root_d).astype(jnp.bfloat16)
    cosine, sine = rotary_tables(length, HD)
    allowed = allowed_pairs(token_ids)
    query_cols = QH * HD // N_TP
    query_heads = QH // N_TP
    query_parts = w_query.reshape(D, N_TP, query_cols).transpose(1, 0, 2)
    out_parts = w_out.reshape(N_TP, query_cols, D)

    def one_shard(totals, inputs):
        out_sum, kv_sum = totals
        wq_part, wo_part, shard_index = inputs
        query_raw = jnp.dot(normed, wq_part, preferred_element_type=jnp.float32) / root_d
        kv_head = shard_index * query_heads // (QH // KVH)
        key_raw = lax.dynamic_slice_in_dim(keyval, kv_head * HD, HD, 1)
        values = lax.dynamic_slice_in_dim(keyval, KVH * HD + kv_head * HD, HD, 1)

        def attend(query_in, key_in, value_in):
            return heads_forward(query_in, key_in, value_in, q_gain, k_gain, cosine, sine, allowed)
        head_mix, pullback = jax.vjp(attend, query_raw, key_raw, values)
        rounded = (jnp.dot(head_mix, wo_part, preferred_element_type=jnp.float32) / root_q).astype(jnp.bfloat16)
        rounded = lax.optimization_barrier(rounded)
        grad_part = jnp.dot(head_mix.T, cotangent, preferred_element_type=jnp.float32) / root_q
        mix_grad = (jnp.dot(cotangent, wo_part.T, preferred_element_type=jnp.float32) / root_q).astype(jnp.bfloat16)
        d_query, d_key, d_value = pullback(mix_grad)
        grad_qpart = jnp.dot(normed.T, d_query.astype(jnp.bfloat16), preferred_element_type=jnp.float32) / root_d
        kv_partial = jnp.zeros((length, 2 * KVH * HD), jnp.float32)
        zero_index = jnp.zeros((), jnp.int32)
        kv_partial = lax.dynamic_update_slice(kv_partial, d_key.astype(jnp.float32), (zero_index, (kv_head * HD).astype(jnp.int32)))
        kv_partial = lax.dynamic_update_slice(kv_partial, d_value.astype(jnp.float32), (zero_index, (KVH * HD + kv_head * HD).astype(jnp.int32)))
        return ((out_sum + rounded.astype(jnp.float32), kv_sum + kv_partial), (grad_qpart, grad_part))
    start_totals = (jnp.zeros((length, D), jnp.float32), jnp.zeros((length, 2 * KVH * HD), jnp.float32))
    shard_ids = jnp.arange(N_TP, dtype=jnp.int32)
    (out_sum, kv_sum), (grad_qparts, grad_oparts) = lax.scan(one_shard, start_totals, (query_parts, out_parts, shard_ids))
    attended = out_sum.astype(jnp.bfloat16)
    grad_query = grad_qparts.transpose(1, 0, 2).reshape(D, QH * HD)
    grad_out = grad_oparts.reshape(QH * HD, D)
    grad_keyval = jnp.dot(kv_sum.astype(jnp.bfloat16).T, normed, preferred_element_type=jnp.float32) / root_d
    stepped_query, new_m_query = advance(w_query, m_query, grad_query, step_rate)
    stepped_keyval, new_m_keyval = advance(w_keyval, m_keyval, grad_keyval, step_rate)
    stepped_out, new_m_out = advance(w_out, m_out, grad_out, step_rate)
    return (attended, stepped_query, stepped_keyval, stepped_out, new_m_query, new_m_keyval, new_m_out)

def reference(tokens, token_ids, cotangent, step_index, norm_gain, q_gain, k_gain, w_query, w_keyval, w_out, m_query, m_keyval, m_out):
    step_rate = warm_rate(step_index)

    def per_group(inputs):
        return group_window(*inputs, norm_gain, q_gain, k_gain, step_rate)
    results = lax.map(per_group, (tokens, token_ids, cotangent, w_query, w_keyval, w_out, m_query, m_keyval, m_out))
    attended, stepped_query, stepped_keyval, stepped_out, new_m_query, new_m_keyval, new_m_out = results
    levels = N_GOSSIP.bit_length() - 1
    offset = jnp.left_shift(jnp.int32(1), (step_index[0] % levels).astype(jnp.int32))
    partner_order = ((jnp.arange(N_GOSSIP, dtype=jnp.int32) + offset) % N_GOSSIP).astype(jnp.int32)

    def average(stepped):
        partner = jnp.take(stepped, partner_order, axis=0)
        return ((stepped.astype(jnp.float32) + partner.astype(jnp.float32)) * 0.5).astype(jnp.bfloat16)
    return (attended, average(stepped_query), average(stepped_keyval), average(stepped_out), new_m_query, new_m_keyval, new_m_out)
```

```python
from functools import partial
import math

import jax
import jax.numpy as jnp
from jax import lax
from jax.experimental import pallas as pl
from jax.experimental.pallas import tpu as pltpu
from jax.sharding import PartitionSpec as P

D = 5120
HD = 128
QH = 32
KVH = 4
S = 1024
ROWS = 64
QUART = 256
VMEM = 36 << 20
COST = pl.CostEstimate(flops=1, bytes_accessed=1, transcendentals=0)
ROOT_D = math.sqrt(D)
ROOT_Q = math.sqrt(QH * HD)
SCALE = 1.0 / math.sqrt(HD)

norm_eps = 1e-06
rope_base = 1000000.0
end_token = 151643
peak_rate = 0.2
momentum_keep = 0.9

BF16 = jnp.bfloat16
F32 = jnp.float32

NEAR = ((0, 0), (0, 1), (0, 3), (1, 0))
FAR = ((1, 1), (1, 3), (0, 2), (1, 2))


def tp_of(y, x, core):
    return (y % 2) * 8 + (x % 4) * 2 + core % 2


def tp_perm(x, move):
    pairs = []
    for y in range(2):
        for i in range(4):
            for core in range(2):
                pairs.append((tp_of(y, i, core), tp_of(*move(y, i, core))))
    return lax.ppermute(x, "tp", pairs)


def x_plus(v):
    return tp_perm(v, lambda y, i, c: (y, i + 1, c))


def x_minus(v):
    return tp_perm(v, lambda y, i, c: (y, i + 3, c))


def x_far(v):
    return tp_perm(v, lambda y, i, c: (y, i + 2, c))


def y_swap(v):
    return tp_perm(v, lambda y, i, c: (y + 1, i, c))


def core_swap(v):
    return tp_perm(v, lambda y, i, c: (y, i, c + 1))


def from_partner(v, offset):
    count = lax.axis_size("gossip")
    return lax.ppermute(v, "gossip", [(i, (i - offset) % count) for i in range(count)])


def phase(*values):
    return lax.optimization_barrier(values)


def stack(*parts):
    return jnp.concatenate(parts, axis=0)


def blocks_of(quarter):
    return [quarter[i * ROWS : (i + 1) * ROWS] for i in range(4)]


def add(*parts):
    total = parts[0].astype(F32)
    for part in parts[1:]:
        total = total + part.astype(F32)
    return total.astype(BF16)


def kv_users(v, r):
    def move(y, i, c):
        return (i // 2, 2 * (i % 2) + (y + r // 2) % 2, (c + r % 2) % 2)

    return tp_perm(v, move)


def kv_owners(v, r):
    def move(y, i, c):
        return ((i % 2 + r // 2) % 2, y * 2 + i // 2, (c + r % 2) % 2)

    return tp_perm(v, move)


def warm_rate(step_index):
    return peak_rate * (step_index[0] + 1).astype(F32) / 1000.0


def normalize(token_rows, gain):
    floats = token_rows.astype(F32)
    scale = lax.rsqrt(jnp.mean(floats * floats, axis=-1, keepdims=True) + norm_eps)
    return (floats * scale * gain).astype(BF16)


def inverse_freq():
    return rope_base ** (-2.0 * jnp.arange(HD // 2, dtype=F32) / HD)


def dot(a, b, dims):
    return lax.dot_general(a, b, (dims, ((), ())), preferred_element_type=F32)


def spec(shape, index):
    return pl.BlockSpec(shape, index)


def fwd_kernel(
    q_ref, kt_ref, vt_ref, cq_ref, sq_ref, ck_ref, sk_ref, lo_ref, hi_ref, qg_ref, kg_ref,
    mix_ref, p_ref, qr_ref, krt_ref,
):
    half = HD // 2

    @pl.when((pl.program_id(0) == 0) & (pl.program_id(1) == 0))
    def _():
        key = kt_ref[...].astype(F32)
        key = key * lax.rsqrt(jnp.mean(key * key, axis=0, keepdims=True) + norm_eps) * kg_ref[...]
        a, b = key[:half], key[half:]
        cosine, sine = ck_ref[...], sk_ref[...]
        krt_ref[:half] = (a * cosine - b * sine).astype(BF16)
        krt_ref[half:] = (b * cosine + a * sine).astype(BF16)

    query = q_ref[...]
    query = query * lax.rsqrt(jnp.mean(query * query, axis=-1, keepdims=True) + norm_eps)
    query = query * qg_ref[...]
    a, b = query[:, :half], query[:, half:]
    cosine, sine = cq_ref[...], sq_ref[...]
    query_rot = jnp.concatenate([a * cosine - b * sine, b * cosine + a * sine], axis=-1)
    query_rot = query_rot.astype(BF16)
    qr_ref[...] = query_rot
    scores = dot(query_rot, krt_ref[...], ((1,), (0,)))
    place = lax.broadcasted_iota(jnp.int32, scores.shape, 1)
    inside = (place >= lo_ref[...]) & (place <= hi_ref[...])
    weights = jnp.where(inside, jnp.exp(scores * SCALE), 0.0)
    total = jnp.sum(weights, axis=-1, keepdims=True)
    probabilities = (weights * (1.0 / total)).astype(BF16)
    p_ref[0] = probabilities
    mix_ref[...] = dot(probabilities, vt_ref[...], ((1,), (1,))).astype(BF16)


def attention_forward(q, kt, vt, cq, sq, ck, sk, lo, hi, q_gain, k_gain):
    half = HD // 2
    tile = spec((QUART, HD), lambda t, h: (t, h))
    whole = lambda *shape: spec(shape, lambda t, h: (0,) * len(shape))
    column = lambda width: spec((QUART, width), lambda t, h: (t, 0))
    return pl.pallas_call(
        fwd_kernel,
        grid=(4, 2),
        in_specs=[
            tile, whole(HD, S), whole(HD, S), column(half), column(half),
            whole(half, S), whole(half, S), column(1), column(1), whole(1, HD), whole(HD, 1),
        ],
        out_specs=[tile, spec((1, QUART, S), lambda t, h: (h, t, 0)), tile, whole(HD, S)],
        out_shape=[
            jax.ShapeDtypeStruct((S, 2 * HD), BF16),
            jax.ShapeDtypeStruct((2, S, S), BF16),
            jax.ShapeDtypeStruct((S, 2 * HD), BF16),
            jax.ShapeDtypeStruct((HD, S), BF16),
        ],
        compiler_params=pltpu.CompilerParams(vmem_limit_bytes=VMEM),
        cost_estimate=COST,
        name="attention_forward",
    )(q, kt, vt, cq, sq, ck, sk, lo, hi, q_gain.reshape(1, HD), k_gain.reshape(HD, 1))


def bwd_kernel(
    p_ref, do_ref, qr_ref, q_ref, krt_ref, kt_ref, vt_ref, cq_ref, sq_ref, ck_ref, sk_ref,
    qg_ref, kg_ref, dq_ref, dkv_ref, dk_acc, dv_acc,
):
    half = HD // 2
    first = (pl.program_id(0) == 0) & (pl.program_id(1) == 0)
    last = (pl.program_id(0) == 3) & (pl.program_id(1) == 1)

    @pl.when(first)
    def _():
        dk_acc[...] = jnp.zeros_like(dk_acc)
        dv_acc[...] = jnp.zeros_like(dv_acc)

    mix_grad = do_ref[...]
    rounded = p_ref[0]
    prob = rounded.astype(F32)
    dp = dot(mix_grad, vt_ref[...], ((1,), (0,)))
    inner = jnp.sum(prob * dp, axis=-1, keepdims=True)
    ds = (prob * (dp - inner) * SCALE).astype(BF16)
    dq = dot(ds, krt_ref[...], ((1,), (1,))).astype(BF16).astype(F32)
    dv_acc[...] += dot(mix_grad, rounded, ((0,), (0,)))
    dk_acc[...] += dot(qr_ref[...], ds, ((0,), (0,)))
    cosine, sine = cq_ref[...], sq_ref[...]
    da, db = dq[:, :half], dq[:, half:]
    dn = jnp.concatenate([da * cosine + db * sine, db * cosine - da * sine], axis=-1)
    dn = dn * qg_ref[...]
    query = q_ref[...]
    scale = lax.rsqrt(jnp.mean(query * query, axis=-1, keepdims=True) + norm_eps)
    pull = jnp.mean(query * dn, axis=-1, keepdims=True) * scale * scale
    dq_ref[...] = (scale * (dn - query * pull)).astype(BF16)

    @pl.when(last)
    def _():
        dk = dk_acc[...].astype(BF16).astype(F32)
        cosine, sine = ck_ref[...], sk_ref[...]
        da, db = dk[:half], dk[half:]
        dn = jnp.concatenate([da * cosine + db * sine, db * cosine - da * sine], axis=0)
        dn = dn * kg_ref[...]
        key = kt_ref[...].astype(F32)
        scale = lax.rsqrt(jnp.mean(key * key, axis=0, keepdims=True) + norm_eps)
        pull = jnp.mean(key * dn, axis=0, keepdims=True) * scale * scale
        dkv_ref[:HD] = (scale * (dn - key * pull)).astype(BF16)
        dkv_ref[HD:] = dv_acc[...].astype(BF16)


def attention_backward(p, do, qr, q, krt, kt, vt, cq, sq, ck, sk, q_gain, k_gain):
    half = HD // 2
    tile = spec((QUART, HD), lambda t, h: (t, h))
    whole = lambda *shape: spec(shape, lambda t, h: (0,) * len(shape))
    column = lambda width: spec((QUART, width), lambda t, h: (t, 0))
    return pl.pallas_call(
        bwd_kernel,
        grid=(4, 2),
        in_specs=[
            spec((1, QUART, S), lambda t, h: (h, t, 0)), tile, tile, tile,
            whole(HD, S), whole(HD, S), whole(HD, S), column(half), column(half),
            whole(half, S), whole(half, S), whole(1, HD), whole(HD, 1),
        ],
        out_specs=[tile, whole(2 * HD, S)],
        out_shape=[
            jax.ShapeDtypeStruct((S, 2 * HD), BF16),
            jax.ShapeDtypeStruct((2 * HD, S), BF16),
        ],
        scratch_shapes=[pltpu.VMEM((HD, S), F32), pltpu.VMEM((HD, S), F32)],
        compiler_params=pltpu.CompilerParams(vmem_limit_bytes=VMEM),
        cost_estimate=COST,
        name="attention_backward",
    )(
        p, do, qr, q, krt, kt, vt, cq, sq, ck, sk, q_gain.reshape(1, HD), k_gain.reshape(HD, 1)
    )


def stepped_values(weight, moment, gradient, rate):
    new_moment = momentum_keep * moment.astype(F32) + gradient
    return (weight.astype(F32) - rate * new_moment).astype(BF16), new_moment.astype(BF16)


def product(refs, g_ref, by_rows):
    total, start = None, 0
    for ref in refs:
        span = slice(start, start + ref.shape[0])
        start += ref.shape[0]
        if by_rows:
            term = dot(g_ref[:, span], ref[...], ((1,), (0,)))
        else:
            term = dot(ref[...], g_ref[span], ((0,), (0,)))
        total = term if total is None else total + term
    return total


def step_kernel(count, by_rows, root, rate_ref, *refs):
    g_ref, w_ref, m_ref, stepped_ref, moment_ref = refs[count:]
    gradient = product(refs[:count], g_ref, by_rows) * (1.0 / root)
    stepped_ref[...], moment_ref[...] = stepped_values(
        w_ref[...], m_ref[...], gradient, rate_ref[0]
    )


def partner_kernel(count, by_rows, root, rate_ref, *refs):
    g_ref, base_ref, stepped_ref, avg_ref = refs[count:]
    scaled = product(refs[:count], g_ref, by_rows) * (rate_ref[0] * (1.0 / root))
    partner = base_ref[...].astype(F32) - scaled
    avg_ref[...] = ((stepped_ref[...].astype(F32) + partner) * 0.5).astype(BF16)


def over_width(kernel, rate, parts, factor, first, second, by_rows, root, outs, name, width=512):
    part = [spec((p.shape[0], width), lambda j: (0, j)) for p in parts]
    if by_rows:
        tile = spec((first.shape[0], width), lambda j: (0, j))
    else:
        tile = spec((width, first.shape[1]), lambda j: (j, 0))
    shape = jax.ShapeDtypeStruct(first.shape, BF16)
    return pl.pallas_call(
        partial(kernel, len(parts), by_rows, root),
        grid=(D // width,),
        in_specs=[pl.BlockSpec(memory_space=pltpu.SMEM)] + part
        + [spec(factor.shape, lambda j: (0, 0)), tile, tile],
        out_specs=[tile] * outs,
        out_shape=[shape] * outs,
        compiler_params=pltpu.CompilerParams(vmem_limit_bytes=VMEM),
        cost_estimate=COST,
        name=name,
    )(rate, *parts, factor, first, second)


def query_kernel(root, rate_ref, n0, n1, n2, n3, g_ref, w_ref, m_ref, low_ref, high_ref, moment_ref):
    gradient = product((n0, n1, n2, n3), g_ref, False) * (1.0 / root)
    stepped, moment_ref[...] = stepped_values(w_ref[...], m_ref[...], gradient, rate_ref[0])
    middle = pl.num_programs(0) // 2

    @pl.when(pl.program_id(0) < middle)
    def _():
        low_ref[...] = stepped

    @pl.when(pl.program_id(0) >= middle)
    def _():
        high_ref[...] = stepped


def halves(width, cols, steps):
    middle = steps // 2
    low = spec((width, cols), lambda j: (jnp.minimum(j, middle - 1), 0))
    high = spec((width, cols), lambda j: (jnp.maximum(j - middle, 0), 0))
    return low, high


def step_query(rate, parts, grad, weight, moment, width=512):
    cols = weight.shape[1]
    steps = D // width
    tile = spec((width, cols), lambda j: (j, 0))
    half = jax.ShapeDtypeStruct((D // 2, cols), BF16)
    return pl.pallas_call(
        partial(query_kernel, ROOT_D),
        grid=(steps,),
        in_specs=[pl.BlockSpec(memory_space=pltpu.SMEM)]
        + [spec((QUART, width), lambda j: (0, j))] * 4
        + [spec(grad.shape, lambda j: (0, 0)), tile, tile],
        out_specs=[*halves(width, cols, steps), tile],
        out_shape=[half, half, jax.ShapeDtypeStruct(weight.shape, BF16)],
        compiler_params=pltpu.CompilerParams(vmem_limit_bytes=VMEM),
        cost_estimate=COST,
        name="step_query",
    )(rate, *parts, grad, weight, moment)


def average_kernel(low, high, partner_low, partner_high, out):
    middle = pl.num_programs(0) // 2

    @pl.when(pl.program_id(0) < middle)
    def _():
        out[...] = average(low[...], partner_low[...])

    @pl.when(pl.program_id(0) >= middle)
    def _():
        out[...] = average(high[...], partner_high[...])


def average_halves(low, high, partner_low, partner_high, width=640):
    cols = low.shape[1]
    steps = D // width
    return pl.pallas_call(
        average_kernel,
        grid=(steps,),
        in_specs=[*halves(width, cols, steps)] * 2,
        out_specs=spec((width, cols), lambda j: (j, 0)),
        out_shape=jax.ShapeDtypeStruct((D, cols), BF16),
        compiler_params=pltpu.CompilerParams(vmem_limit_bytes=VMEM),
        cost_estimate=COST,
        name="average_query",
    )(low, high, partner_low, partner_high)


def project_kernel(count, *refs):
    parts, (wq_ref, wkv_ref), outs = refs[:count], refs[count : count + 2], refs[count + 2 :]
    if count == 1:
        rows_ref = parts[0]
        q_ref, kv_ref = outs
    else:
        rows_ref, q_ref, kv_ref = outs
        for i, part in enumerate(parts):
            rows_ref[i * ROWS : (i + 1) * ROWS] = part[...]
    q_ref[...] = dot(rows_ref[...], wq_ref[...], ((1,), (0,))) * (1.0 / ROOT_D)
    kv = dot(wkv_ref[...], rows_ref[...], ((1,), (1,))) * (1.0 / ROOT_D)
    kv_ref[...] = kv.astype(BF16)


def project(parts, w_query, w_keyval):
    vmem = pl.BlockSpec(memory_space=pltpu.VMEM)
    shapes = [
        jax.ShapeDtypeStruct((QUART, w_query.shape[1]), F32),
        jax.ShapeDtypeStruct((w_keyval.shape[0], QUART), BF16),
    ]
    if len(parts) > 1:
        shapes = [jax.ShapeDtypeStruct((QUART, D), BF16)] + shapes
    return pl.pallas_call(
        partial(project_kernel, len(parts)),
        in_specs=[vmem] * (len(parts) + 2),
        out_specs=[vmem] * len(shapes),
        out_shape=shapes,
        compiler_params=pltpu.CompilerParams(vmem_limit_bytes=VMEM),
        cost_estimate=COST,
        name="project",
    )(*parts, w_query, w_keyval)


def mix_grad_kernel(order_ref, cot_ref, w_ref, out_ref, acc_ref):
    step = pl.program_id(0)

    @pl.when(step == 0)
    def _():
        acc_ref[...] = jnp.zeros_like(acc_ref)

    acc_ref[...] += dot(cot_ref[...], w_ref[...], ((1,), (1,)))

    @pl.when(step == pl.num_programs(0) - 1)
    def _():
        for i in range(S // ROWS):
            rows = acc_ref[pl.ds(pl.multiple_of(order_ref[i] * ROWS, ROWS), ROWS)]
            out_ref[i * ROWS : (i + 1) * ROWS] = (rows * (1.0 / ROOT_Q)).astype(BF16)


def mix_gradient(order, cot_rows, w_out, width=512):
    cols = w_out.shape[0]
    return pl.pallas_call(
        mix_grad_kernel,
        grid=(D // width,),
        in_specs=[
            pl.BlockSpec(memory_space=pltpu.SMEM),
            spec((S, width), lambda j: (0, j)),
            spec((cols, width), lambda j: (0, j)),
        ],
        out_specs=spec((S, cols), lambda j: (0, 0)),
        out_shape=jax.ShapeDtypeStruct((S, cols), BF16),
        scratch_shapes=[pltpu.VMEM((S, cols), F32)],
        compiler_params=pltpu.CompilerParams(vmem_limit_bytes=VMEM),
        cost_estimate=COST,
        name="mix_gradient",
    )(order, cot_rows, w_out)


def terms_kernel(mix_ref, w_ref, *outs):
    for i, out in enumerate(outs):
        term = dot(mix_ref[i * QUART : (i + 1) * QUART], w_ref[...], ((1,), (0,)))
        out[...] = (term * (1.0 / ROOT_Q)).astype(BF16)


def output_terms(mix, w_out, width=512):
    cols = w_out.shape[0]
    return pl.pallas_call(
        terms_kernel,
        grid=(D // width,),
        in_specs=[spec((S, cols), lambda j: (0, 0)), spec((cols, width), lambda j: (0, j))],
        out_specs=[spec((QUART, width), lambda j: (0, j))] * 4,
        out_shape=[jax.ShapeDtypeStruct((QUART, D), BF16)] * 4,
        compiler_params=pltpu.CompilerParams(vmem_limit_bytes=VMEM),
        cost_estimate=COST,
        name="output_terms",
    )(mix, w_out)


def average(stepped, partner):
    return ((stepped.astype(F32) + partner.astype(F32)) * 0.5).astype(BF16)


def body(
    offset,
    tokens, token_ids, cotangent, rate, norm_gain, q_gain, k_gain,
    w_query, w_keyval, w_out, m_query, m_keyval, m_out,
):
    me = lax.axis_index("tp")
    y, x, core = me // 8, (me // 2) % 4, me % 2

    order = []
    for blocks in (NEAR, FAR):
        for other in (0, 1):
            order += [tp_of(y + dy, x + dx, core + other) for dy, dx in blocks]
    order = jnp.stack(order).astype(jnp.int32)
    places = jnp.arange(S, dtype=jnp.int32)
    held = (order[:, None] * ROWS + jnp.arange(ROWS, dtype=jnp.int32)[None]).reshape(S)
    match = held[:, None] == places[None, :]
    closing = (token_ids == end_token).astype(jnp.int32)
    begins = jnp.concatenate([jnp.ones((1,), jnp.int32), closing[:-1]])
    document_start = lax.cummax(jnp.where(begins > 0, places, 0))
    lo = jnp.sum(jnp.where(match, document_start[None, :], 0), axis=1, keepdims=True)
    hi = held[:, None]
    to_whole = match.astype(BF16)
    held_angles = held.astype(F32)[:, None] * inverse_freq()[None]
    whole_angles = inverse_freq()[:, None] * places.astype(F32)[None]
    cq, sq = jnp.cos(held_angles), jnp.sin(held_angles)
    ck, sk = jnp.cos(whole_angles), jnp.sin(whole_angles)

    near_y = offset == 1
    own = normalize(tokens, norm_gain)
    base = (w_out.astype(F32) - rate[0] * (momentum_keep * m_out.astype(F32))).astype(BF16)
    base = blocks_of(base)
    right, left, across, opposite = x_plus(own), x_minus(own), y_swap(own), x_far(own)
    cot_rows = lax.all_gather(cotangent, "tp", axis=0, tiled=True)
    partner_cot = from_partner(cotangent, offset)
    own, right, left, across, opposite, partner_cot, lo, hi, to_whole, cq, sq, ck, sk, *base = phase(
        own, right, left, across, opposite, partner_cot, lo, hi, to_whole, cq, sq, ck, sk, *base
    )

    across_right, across_left, across_opposite = x_plus(across), x_minus(across), y_swap(opposite)
    if not near_y:
        base[0] = from_partner(base[0], offset)
    near, query_near, kv_near = project([own, left, right, across], w_query, w_keyval)
    near_other = core_swap(near)
    query_near_other, kv_near_other = project([near_other], w_query, w_keyval)
    (
        across_left, across_right, across_opposite, query_near_other, kv_near_other, *base
    ) = phase(across_left, across_right, across_opposite, query_near_other, kv_near_other, *base)

    if not near_y:
        base[1] = from_partner(base[1], offset)
    partner_rows = lax.all_gather(partner_cot, "tp", axis=0, tiled=True)
    far, query_far, kv_far = project(
        [across_left, across_right, opposite, across_opposite], w_query, w_keyval
    )
    far_other = core_swap(far)
    query_far_other, kv_far_other = project([far_other], w_query, w_keyval)
    rows = (near, near_other, far, far_other)
    kv_held = jnp.concatenate([kv_near, kv_near_other, kv_far, kv_far_other], axis=1)
    kv_own = dot(kv_held, to_whole, ((1,), (0,))).astype(BF16)
    kv_own, *base = phase(kv_own, *base)

    arrived = [kv_users(kv_own, r) for r in range(4)]
    if near_y:
        base[0] = from_partner(base[0], offset)
    else:
        base[2] = from_partner(base[2], offset)
    query = stack(query_near, query_near_other, query_far, query_far_other)
    *arrived, query, base[2], base[3] = phase(*arrived, query, base[2], base[3])

    if near_y:
        base[1] = from_partner(base[1], offset)
    else:
        base[3] = from_partner(base[3], offset)
    odd_x, odd_core = x % 2 == 1, core == 1

    def in_order(first, second):
        return stack(jnp.where(odd_core, second, first), jnp.where(odd_core, first, second))

    same, other = in_order(arrived[0], arrived[1]), in_order(arrived[2], arrived[3])
    kt, vt = jnp.where(odd_x, other, same), jnp.where(odd_x, same, other)
    mix, prob, query_rot, krt = attention_forward(
        query, kt, vt, cq, sq, ck, sk, lo, hi, q_gain, k_gain
    )
    mix_whole_t = dot(mix, to_whole, ((0,), (0,))).astype(BF16)
    cot_rows, mix, mix_whole_t, *base = phase(cot_rows, mix, mix_whole_t, *base)

    partner_mix = from_partner(mix_whole_t, offset)
    if near_y:
        base[2] = from_partner(base[2], offset)
    mix_grad = mix_gradient(order, cot_rows, w_out)
    query_grad, kv_parts = attention_backward(
        prob, mix_grad, query_rot, query, krt, kt, vt, cq, sq, ck, sk, q_gain, k_gain
    )
    stepped_low, stepped_high, new_m_query = step_query(rate, rows, query_grad, w_query, m_query)
    kv_parts, stepped_low, stepped_high, mix, mix_whole_t, partner_mix, *base = phase(
        kv_parts, stepped_low, stepped_high, mix, mix_whole_t, partner_mix, *base
    )

    partner_low = from_partner(stepped_low, offset)
    kv_split = kv_parts.reshape(2, 2, ROWS, S)
    received = []
    for r in range(4):
        kind, which = (x + r // 2) % 2, (core + r % 2) % 2
        piece = lax.dynamic_slice(kv_split, (kind, which, 0, 0), (1, 1, ROWS, S))
        received.append(kv_owners(piece.reshape(ROWS, S), r))
    terms = output_terms(mix, w_out)
    near_in, far_in = core_swap(terms[1]), core_swap(terms[3])
    stepped_out, new_m_out = over_width(
        step_kernel, rate, [cot_rows], mix_whole_t, w_out, m_out, True, ROOT_Q, 2, "step_out"
    )
    partner_low, near_in, far_in, stepped_out, stepped_high, *received = phase(
        partner_low, near_in, far_in, stepped_out, stepped_high, *received
    )

    partner_high = from_partner(stepped_high, offset)
    if near_y:
        base[3] = from_partner(base[3], offset)
    far_sum, near_sum = add(terms[2], far_in), add(terms[0], near_in)
    s_left, s_right, s_opposite, s_across = blocks_of(far_sum)
    t_own, t_left, t_right, t_across = blocks_of(near_sum)
    left_in, right_in, across_in = x_plus(s_left), x_minus(s_right), y_swap(s_across)
    t_right_in, t_left_in = x_minus(t_right), x_plus(t_left)
    keyval_grad = add(*received)
    keyval_grad = dot(keyval_grad, to_whole, ((1,), (1,))).astype(BF16)
    stepped_keyval, new_m_keyval = over_width(
        step_kernel, rate, rows, keyval_grad, w_keyval, m_keyval, True, ROOT_D, 2, "step_keyval"
    )
    (
        partner_high, stepped_keyval, left_in, right_in, across_in, t_right_in, t_left_in, stepped_out
    ) = phase(
        partner_high, stepped_keyval, left_in, right_in, across_in, t_right_in, t_left_in, stepped_out
    )

    partner_keyval = from_partner(stepped_keyval, offset)
    t_opposite_in = x_far(add(s_opposite, across_in))
    t_across_in = y_swap(add(t_across, left_in, right_in))
    avg_query = average_halves(stepped_low, stepped_high, partner_low, partner_high)
    (avg_out,) = over_width(
        partner_kernel, rate, [partner_rows], partner_mix, stack(*base), stepped_out,
        True, ROOT_Q, 1, "average_out",
    )
    attended = add(t_own, t_across_in, t_right_in, t_left_in, t_opposite_in)
    return (
        attended,
        avg_query,
        average(stepped_keyval, partner_keyval),
        avg_out,
        new_m_query,
        new_m_keyval,
        new_m_out,
    )


def per_device(
    tokens, token_ids, cotangent, step_index, norm_gain, q_gain, k_gain,
    w_query, w_keyval, w_out, m_query, m_keyval, m_out,
):
    rate = warm_rate(step_index).reshape(1)
    levels = lax.axis_size("gossip").bit_length() - 1
    branches = [partial(body, 1 << level) for level in range(levels)]
    outs = lax.switch(
        step_index[0] % levels, branches,
        tokens[0], token_ids[0], cotangent[0], rate, norm_gain, q_gain, k_gain,
        w_query[0], w_keyval[0], w_out[0], m_query[0], m_keyval[0], m_out[0],
    )
    return tuple(out[None] for out in outs)


def solution(mesh):
    placed = (
        P("gossip", "tp", None),
        P("gossip", None),
        P("gossip", "tp", None),
        P(),
        P(),
        P(),
        P(),
        P("gossip", None, "tp"),
        P("gossip", "tp", None),
        P("gossip", "tp", None),
        P("gossip", None, "tp"),
        P("gossip", "tp", None),
        P("gossip", "tp", None),
    )
    return jax.shard_map(
        per_device,
        mesh=mesh,
        in_specs=placed,
        out_specs=(
            P("gossip", "tp", None),
            P("gossip", None, "tp"),
            P("gossip", "tp", None),
            P("gossip", "tp", None),
            P("gossip", None, "tp"),
            P("gossip", "tp", None),
            P("gossip", "tp", None),
        ),
        check_vma=False,
    )
```

```python
from functools import partial
import math

import jax
import jax.numpy as jnp
from jax import lax
from jax.experimental import pallas as pl
from jax.experimental.pallas import tpu as pltpu
from jax.sharding import PartitionSpec as P

D = 5120
HD = 128
QH = 32
KVH = 4
S = 1024
ROWS = 64
QUART = 256
VMEM = 36 << 20
VMEM_ALL = 58 << 20
COST = pl.CostEstimate(flops=1, bytes_accessed=1, transcendentals=0)
ROOT_D = math.sqrt(D)
ROOT_Q = math.sqrt(QH * HD)
SCALE = 1.0 / math.sqrt(HD)

norm_eps = 1e-06
rope_base = 1000000.0
end_token = 151643
peak_rate = 0.2
momentum_keep = 0.9

BF16 = jnp.bfloat16
F32 = jnp.float32

NEAR = ((0, 0), (0, 1), (0, 3), (1, 0))
FAR = ((1, 1), (1, 3), (0, 2), (1, 2))


def tp_of(y, x, core):
    return (y % 2) * 8 + (x % 4) * 2 + core % 2


def tp_perm(x, move):
    pairs = []
    for y in range(2):
        for i in range(4):
            for core in range(2):
                pairs.append((tp_of(y, i, core), tp_of(*move(y, i, core))))
    return lax.ppermute(x, "tp", pairs)


def x_plus(v):
    return tp_perm(v, lambda y, i, c: (y, i + 1, c))


def x_minus(v):
    return tp_perm(v, lambda y, i, c: (y, i + 3, c))


def x_far(v):
    return tp_perm(v, lambda y, i, c: (y, i + 2, c))


def y_swap(v):
    return tp_perm(v, lambda y, i, c: (y + 1, i, c))


def core_swap(v):
    return tp_perm(v, lambda y, i, c: (y, i, c + 1))


def from_partner(v, offset):
    count = lax.axis_size("gossip")
    return lax.ppermute(v, "gossip", [(i, (i - offset) % count) for i in range(count)])


def phase(*values):
    return lax.optimization_barrier(values)


def stack(*parts):
    return jnp.concatenate(parts, axis=0)


def blocks_of(quarter):
    return [quarter[i * ROWS : (i + 1) * ROWS] for i in range(4)]


def add(*parts):
    total = parts[0].astype(F32)
    for part in parts[1:]:
        total = total + part.astype(F32)
    return total.astype(BF16)


def kv_users(v, r):
    def move(y, i, c):
        return (i // 2, 2 * (i % 2) + (y + r // 2) % 2, (c + r % 2) % 2)

    return tp_perm(v, move)


def kv_owners(v, r):
    def move(y, i, c):
        return ((i % 2 + r // 2) % 2, y * 2 + i // 2, (c + r % 2) % 2)

    return tp_perm(v, move)


def warm_rate(step_index):
    return peak_rate * (step_index[0] + 1).astype(F32) / 1000.0


def normalize(token_rows, gain):
    floats = token_rows.astype(F32)
    scale = lax.rsqrt(jnp.mean(floats * floats, axis=-1, keepdims=True) + norm_eps)
    return (floats * scale * gain).astype(BF16)


def inverse_freq():
    return rope_base ** (-2.0 * jnp.arange(HD // 2, dtype=F32) / HD)


def dot(a, b, dims):
    return lax.dot_general(a, b, (dims, ((), ())), preferred_element_type=F32)


def spec(shape, index):
    return pl.BlockSpec(shape, index)


def fwd_kernel(
    q_ref, kt_ref, vt_ref, cq_ref, sq_ref, ck_ref, sk_ref, lo_ref, hi_ref, qg_ref, kg_ref,
    mix_ref, p_ref, qr_ref, krt_ref,
):
    half = HD // 2

    @pl.when((pl.program_id(0) == 0) & (pl.program_id(1) == 0))
    def _():
        key = kt_ref[...].astype(F32)
        key = key * lax.rsqrt(jnp.mean(key * key, axis=0, keepdims=True) + norm_eps) * kg_ref[...]
        a, b = key[:half], key[half:]
        cosine, sine = ck_ref[...], sk_ref[...]
        krt_ref[:half] = (a * cosine - b * sine).astype(BF16)
        krt_ref[half:] = (b * cosine + a * sine).astype(BF16)

    query = q_ref[...]
    query = query * lax.rsqrt(jnp.mean(query * query, axis=-1, keepdims=True) + norm_eps)
    query = query * qg_ref[...]
    a, b = query[:, :half], query[:, half:]
    cosine, sine = cq_ref[...], sq_ref[...]
    query_rot = jnp.concatenate([a * cosine - b * sine, b * cosine + a * sine], axis=-1)
    query_rot = query_rot.astype(BF16)
    qr_ref[...] = query_rot
    scores = dot(query_rot, krt_ref[...], ((1,), (0,)))
    place = lax.broadcasted_iota(jnp.int32, scores.shape, 1)
    inside = (place >= lo_ref[...]) & (place <= hi_ref[...])
    weights = jnp.where(inside, jnp.exp(scores * SCALE), 0.0)
    total = jnp.sum(weights, axis=-1, keepdims=True)
    probabilities = (weights * (1.0 / total)).astype(BF16)
    p_ref[0] = probabilities
    mix_ref[...] = dot(probabilities, vt_ref[...], ((1,), (1,))).astype(BF16)


def attention_forward(q, kt, vt, cq, sq, ck, sk, lo, hi, q_gain, k_gain):
    half = HD // 2
    tile = spec((QUART, HD), lambda t, h: (t, h))
    whole = lambda *shape: spec(shape, lambda t, h: (0,) * len(shape))
    column = lambda width: spec((QUART, width), lambda t, h: (t, 0))
    return pl.pallas_call(
        fwd_kernel,
        grid=(4, 2),
        in_specs=[
            tile, whole(HD, S), whole(HD, S), column(half), column(half),
            whole(half, S), whole(half, S), column(1), column(1), whole(1, HD), whole(HD, 1),
        ],
        out_specs=[tile, spec((1, QUART, S), lambda t, h: (h, t, 0)), tile, whole(HD, S)],
        out_shape=[
            jax.ShapeDtypeStruct((S, 2 * HD), BF16),
            jax.ShapeDtypeStruct((2, S, S), BF16),
            jax.ShapeDtypeStruct((S, 2 * HD), BF16),
            jax.ShapeDtypeStruct((HD, S), BF16),
        ],
        compiler_params=pltpu.CompilerParams(vmem_limit_bytes=VMEM),
        cost_estimate=COST,
        name="attention_forward",
    )(q, kt, vt, cq, sq, ck, sk, lo, hi, q_gain.reshape(1, HD), k_gain.reshape(HD, 1))


def bwd_kernel(
    p_ref, do_ref, qr_ref, q_ref, krt_ref, kt_ref, vt_ref, cq_ref, sq_ref, ck_ref, sk_ref,
    qg_ref, kg_ref, dq_ref, dkv_ref, dk_acc, dv_acc,
):
    half = HD // 2
    first = (pl.program_id(0) == 0) & (pl.program_id(1) == 0)
    last = (pl.program_id(0) == 3) & (pl.program_id(1) == 1)

    @pl.when(first)
    def _():
        dk_acc[...] = jnp.zeros_like(dk_acc)
        dv_acc[...] = jnp.zeros_like(dv_acc)

    mix_grad = do_ref[...]
    rounded = p_ref[0]
    prob = rounded.astype(F32)
    dp = dot(mix_grad, vt_ref[...], ((1,), (0,)))
    inner = jnp.sum(prob * dp, axis=-1, keepdims=True)
    ds = (prob * (dp - inner) * SCALE).astype(BF16)
    dq = dot(ds, krt_ref[...], ((1,), (1,))).astype(BF16).astype(F32)
    dv_acc[...] += dot(mix_grad, rounded, ((0,), (0,)))
    dk_acc[...] += dot(qr_ref[...], ds, ((0,), (0,)))
    cosine, sine = cq_ref[...], sq_ref[...]
    da, db = dq[:, :half], dq[:, half:]
    dn = jnp.concatenate([da * cosine + db * sine, db * cosine - da * sine], axis=-1)
    dn = dn * qg_ref[...]
    query = q_ref[...]
    scale = lax.rsqrt(jnp.mean(query * query, axis=-1, keepdims=True) + norm_eps)
    pull = jnp.mean(query * dn, axis=-1, keepdims=True) * scale * scale
    dq_ref[...] = (scale * (dn - query * pull)).astype(BF16)

    @pl.when(last)
    def _():
        dk = dk_acc[...].astype(BF16).astype(F32)
        cosine, sine = ck_ref[...], sk_ref[...]
        da, db = dk[:half], dk[half:]
        dn = jnp.concatenate([da * cosine + db * sine, db * cosine - da * sine], axis=0)
        dn = dn * kg_ref[...]
        key = kt_ref[...].astype(F32)
        scale = lax.rsqrt(jnp.mean(key * key, axis=0, keepdims=True) + norm_eps)
        pull = jnp.mean(key * dn, axis=0, keepdims=True) * scale * scale
        dkv_ref[:HD] = (scale * (dn - key * pull)).astype(BF16)
        dkv_ref[HD:] = dv_acc[...].astype(BF16)


def attention_backward(p, do, qr, q, krt, kt, vt, cq, sq, ck, sk, q_gain, k_gain):
    half = HD // 2
    tile = spec((QUART, HD), lambda t, h: (t, h))
    whole = lambda *shape: spec(shape, lambda t, h: (0,) * len(shape))
    column = lambda width: spec((QUART, width), lambda t, h: (t, 0))
    return pl.pallas_call(
        bwd_kernel,
        grid=(4, 2),
        in_specs=[
            spec((1, QUART, S), lambda t, h: (h, t, 0)), tile, tile, tile,
            whole(HD, S), whole(HD, S), whole(HD, S), column(half), column(half),
            whole(half, S), whole(half, S), whole(1, HD), whole(HD, 1),
        ],
        out_specs=[tile, whole(2 * HD, S)],
        out_shape=[
            jax.ShapeDtypeStruct((S, 2 * HD), BF16),
            jax.ShapeDtypeStruct((2 * HD, S), BF16),
        ],
        scratch_shapes=[pltpu.VMEM((HD, S), F32), pltpu.VMEM((HD, S), F32)],
        compiler_params=pltpu.CompilerParams(vmem_limit_bytes=VMEM_ALL),
        cost_estimate=COST,
        name="attention_backward",
    )(
        p, do, qr, q, krt, kt, vt, cq, sq, ck, sk, q_gain.reshape(1, HD), k_gain.reshape(HD, 1)
    )


def stepped_values(weight, moment, gradient, rate):
    new_moment = momentum_keep * moment.astype(F32) + gradient
    return (weight.astype(F32) - rate * new_moment).astype(BF16), new_moment.astype(BF16)


def product(refs, g_ref, by_rows):
    total, start = None, 0
    for ref in refs:
        span = slice(start, start + ref.shape[0])
        start += ref.shape[0]
        if by_rows:
            term = dot(g_ref[:, span], ref[...], ((1,), (0,)))
        else:
            term = dot(ref[...], g_ref[span], ((0,), (0,)))
        total = term if total is None else total + term
    return total


def step_kernel(count, by_rows, root, rate_ref, *refs):
    g_ref, w_ref, m_ref, stepped_ref, moment_ref = refs[count:]
    gradient = product(refs[:count], g_ref, by_rows) * (1.0 / root)
    stepped_ref[...], moment_ref[...] = stepped_values(
        w_ref[...], m_ref[...], gradient, rate_ref[0]
    )


def partner_kernel(count, by_rows, root, rate_ref, *refs):
    g_ref, base_ref, stepped_ref, avg_ref = refs[count:]
    scaled = product(refs[:count], g_ref, by_rows) * (rate_ref[0] * (1.0 / root))
    partner = base_ref[...].astype(F32) - scaled
    avg_ref[...] = ((stepped_ref[...].astype(F32) + partner) * 0.5).astype(BF16)


def over_width(kernel, rate, parts, factor, first, second, by_rows, root, outs, name, width=512):
    part = [spec((p.shape[0], width), lambda j: (0, j)) for p in parts]
    if by_rows:
        tile = spec((first.shape[0], width), lambda j: (0, j))
    else:
        tile = spec((width, first.shape[1]), lambda j: (j, 0))
    shape = jax.ShapeDtypeStruct(first.shape, BF16)
    return pl.pallas_call(
        partial(kernel, len(parts), by_rows, root),
        grid=(D // width,),
        in_specs=[pl.BlockSpec(memory_space=pltpu.SMEM)] + part
        + [spec(factor.shape, lambda j: (0, 0)), tile, tile],
        out_specs=[tile] * outs,
        out_shape=[shape] * outs,
        compiler_params=pltpu.CompilerParams(vmem_limit_bytes=VMEM_ALL if len(parts) == 1 else VMEM),
        cost_estimate=COST,
        name=name,
    )(rate, *parts, factor, first, second)


def project_kernel(count, *refs):
    parts, (wq_ref, wkv_ref), outs = refs[:count], refs[count : count + 2], refs[count + 2 :]
    if count == 1:
        rows_ref = parts[0]
        q_ref, kv_ref = outs
    else:
        rows_ref, q_ref, kv_ref = outs
        for i, part in enumerate(parts):
            rows_ref[i * ROWS : (i + 1) * ROWS] = part[...]
    q_ref[...] = dot(rows_ref[...], wq_ref[...], ((1,), (0,))) * (1.0 / ROOT_D)
    kv = dot(wkv_ref[...], rows_ref[...], ((1,), (1,))) * (1.0 / ROOT_D)
    kv_ref[...] = kv.astype(BF16)


def project(parts, w_query, w_keyval):
    vmem = pl.BlockSpec(memory_space=pltpu.VMEM)
    shapes = [
        jax.ShapeDtypeStruct((QUART, w_query.shape[1]), F32),
        jax.ShapeDtypeStruct((w_keyval.shape[0], QUART), BF16),
    ]
    if len(parts) > 1:
        shapes = [jax.ShapeDtypeStruct((QUART, D), BF16)] + shapes
    return pl.pallas_call(
        partial(project_kernel, len(parts)),
        in_specs=[vmem] * (len(parts) + 2),
        out_specs=[vmem] * len(shapes),
        out_shape=shapes,
        compiler_params=pltpu.CompilerParams(vmem_limit_bytes=VMEM),
        cost_estimate=COST,
        name="project",
    )(*parts, w_query, w_keyval)


def mix_grad_kernel(order_ref, cot_ref, w_ref, out_ref, acc_ref):
    step = pl.program_id(0)

    @pl.when(step == 0)
    def _():
        acc_ref[...] = jnp.zeros_like(acc_ref)

    acc_ref[...] += dot(cot_ref[...], w_ref[...], ((1,), (1,)))

    @pl.when(step == pl.num_programs(0) - 1)
    def _():
        for i in range(S // ROWS):
            rows = acc_ref[pl.ds(pl.multiple_of(order_ref[i] * ROWS, ROWS), ROWS)]
            out_ref[i * ROWS : (i + 1) * ROWS] = (rows * (1.0 / ROOT_Q)).astype(BF16)


def mix_gradient(order, cot_rows, w_out, width=512):
    cols = w_out.shape[0]
    return pl.pallas_call(
        mix_grad_kernel,
        grid=(D // width,),
        in_specs=[
            pl.BlockSpec(memory_space=pltpu.SMEM),
            spec((S, width), lambda j: (0, j)),
            spec((cols, width), lambda j: (0, j)),
        ],
        out_specs=spec((S, cols), lambda j: (0, 0)),
        out_shape=jax.ShapeDtypeStruct((S, cols), BF16),
        scratch_shapes=[pltpu.VMEM((S, cols), F32)],
        compiler_params=pltpu.CompilerParams(vmem_limit_bytes=VMEM_ALL),
        cost_estimate=COST,
        name="mix_gradient",
    )(order, cot_rows, w_out)


def terms_kernel(mix_ref, w_ref, *outs):
    for i, out in enumerate(outs):
        term = dot(mix_ref[i * QUART : (i + 1) * QUART], w_ref[...], ((1,), (0,)))
        out[...] = (term * (1.0 / ROOT_Q)).astype(BF16)


def output_terms(mix, w_out, width=512):
    cols = w_out.shape[0]
    return pl.pallas_call(
        terms_kernel,
        grid=(D // width,),
        in_specs=[spec((S, cols), lambda j: (0, 0)), spec((cols, width), lambda j: (0, j))],
        out_specs=[spec((QUART, width), lambda j: (0, j))] * 4,
        out_shape=[jax.ShapeDtypeStruct((QUART, D), BF16)] * 4,
        compiler_params=pltpu.CompilerParams(vmem_limit_bytes=VMEM_ALL),
        cost_estimate=COST,
        name="output_terms",
    )(mix, w_out)


def average(stepped, partner):
    return ((stepped.astype(F32) + partner.astype(F32)) * 0.5).astype(BF16)


def body(
    offset,
    tokens, token_ids, cotangent, rate, norm_gain, q_gain, k_gain,
    w_query, w_keyval, w_out, m_query, m_keyval, m_out,
):
    me = lax.axis_index("tp")
    y, x, core = me // 8, (me // 2) % 4, me % 2

    order = []
    for blocks in (NEAR, FAR):
        for other in (0, 1):
            order += [tp_of(y + dy, x + dx, core + other) for dy, dx in blocks]
    order = jnp.stack(order).astype(jnp.int32)
    places = jnp.arange(S, dtype=jnp.int32)
    held = (order[:, None] * ROWS + jnp.arange(ROWS, dtype=jnp.int32)[None]).reshape(S)
    match = held[:, None] == places[None, :]
    closing = (token_ids == end_token).astype(jnp.int32)
    begins = jnp.concatenate([jnp.ones((1,), jnp.int32), closing[:-1]])
    document_start = lax.cummax(jnp.where(begins > 0, places, 0))
    lo = jnp.sum(jnp.where(match, document_start[None, :], 0), axis=1, keepdims=True)
    hi = held[:, None]
    to_whole = match.astype(BF16)
    held_angles = held.astype(F32)[:, None] * inverse_freq()[None]
    whole_angles = inverse_freq()[:, None] * places.astype(F32)[None]
    cq, sq = jnp.cos(held_angles), jnp.sin(held_angles)
    ck, sk = jnp.cos(whole_angles), jnp.sin(whole_angles)

    near_y = offset == 1
    own = normalize(tokens, norm_gain)
    base = (w_out.astype(F32) - rate[0] * (momentum_keep * m_out.astype(F32))).astype(BF16)
    base = blocks_of(base)
    right, left, across, opposite = x_plus(own), x_minus(own), y_swap(own), x_far(own)
    partner_cot = from_partner(cotangent, offset)
    (
        own, right, left, across, opposite, partner_cot, lo, hi, to_whole, cq, sq, ck, sk, cotangent, *base
    ) = phase(
        own, right, left, across, opposite, partner_cot, lo, hi, to_whole, cq, sq, ck, sk, cotangent, *base
    )
    cot_rows = lax.all_gather(cotangent, "tp", axis=0, tiled=True)

    across_right, across_left, across_opposite = x_plus(across), x_minus(across), y_swap(opposite)
    if not near_y:
        base[0], base[1] = from_partner(base[0], offset), from_partner(base[1], offset)
    near, query_near, kv_near = project([own, left, right, across], w_query, w_keyval)
    near_other = core_swap(near)
    query_near_other, kv_near_other = project([near_other], w_query, w_keyval)
    (
        across_left, across_right, across_opposite, query_near_other, kv_near_other, *base
    ) = phase(across_left, across_right, across_opposite, query_near_other, kv_near_other, *base)

    partner_rows = lax.all_gather(partner_cot, "tp", axis=0, tiled=True)
    far, query_far, kv_far = project(
        [across_left, across_right, opposite, across_opposite], w_query, w_keyval
    )
    far_other = core_swap(far)
    query_far_other, kv_far_other = project([far_other], w_query, w_keyval)
    rows = (near, near_other, far, far_other)
    kv_held = jnp.concatenate([kv_near, kv_near_other, kv_far, kv_far_other], axis=1)
    kv_own = dot(kv_held, to_whole, ((1,), (0,))).astype(BF16)
    kv_own, *base = phase(kv_own, *base)

    arrived = [kv_users(kv_own, r) for r in range(4)]
    if near_y:
        base[0] = from_partner(base[0], offset)
    else:
        base[2] = from_partner(base[2], offset)
    query = stack(query_near, query_near_other, query_far, query_far_other)
    *arrived, query, base[2], base[3] = phase(*arrived, query, base[2], base[3])

    odd_x, odd_core = x % 2 == 1, core == 1

    def in_order(first, second):
        return stack(jnp.where(odd_core, second, first), jnp.where(odd_core, first, second))

    same, other = in_order(arrived[0], arrived[1]), in_order(arrived[2], arrived[3])
    kt, vt = jnp.where(odd_x, other, same), jnp.where(odd_x, same, other)
    mix, prob, query_rot, krt = attention_forward(
        query, kt, vt, cq, sq, ck, sk, lo, hi, q_gain, k_gain
    )
    mix_whole_t = dot(mix, to_whole, ((0,), (0,))).astype(BF16)
    terms = output_terms(mix, w_out)
    cot_rows, mix_whole_t, prob, *base = phase(cot_rows, mix_whole_t, prob, *base)

    partner_mix = from_partner(mix_whole_t, offset)
    if near_y:
        base[1] = from_partner(base[1], offset)
    else:
        base[3] = from_partner(base[3], offset)
    near_in, far_in = core_swap(terms[1]), core_swap(terms[3])
    mix_grad = mix_gradient(order, cot_rows, w_out)
    query_grad, kv_parts = attention_backward(
        prob, mix_grad, query_rot, query, krt, kt, vt, cq, sq, ck, sk, q_gain, k_gain
    )
    stepped_query, new_m_query = over_width(
        step_kernel, rate, rows, query_grad, w_query, m_query, False, ROOT_D, 2, "step_query"
    )
    kv_parts, stepped_query, mix_whole_t, partner_mix, near_in, far_in, *base = phase(
        kv_parts, stepped_query, mix_whole_t, partner_mix, near_in, far_in, *base
    )

    partner_query = from_partner(stepped_query, offset)
    if near_y:
        base[2] = from_partner(base[2], offset)
    kv_split = kv_parts.reshape(2, 2, ROWS, S)
    received = []
    for r in range(4):
        kind, which = (x + r // 2) % 2, (core + r % 2) % 2
        piece = lax.dynamic_slice(kv_split, (kind, which, 0, 0), (1, 1, ROWS, S))
        received.append(kv_owners(piece.reshape(ROWS, S), r))
    far_sum, near_sum = add(terms[2], far_in), add(terms[0], near_in)
    s_left, s_right, s_opposite, s_across = blocks_of(far_sum)
    t_own, t_left, t_right, t_across = blocks_of(near_sum)
    left_in, right_in, across_in = x_plus(s_left), x_minus(s_right), y_swap(s_across)
    t_right_in, t_left_in = x_minus(t_right), x_plus(t_left)
    stepped_out, new_m_out = over_width(
        step_kernel, rate, [cot_rows], mix_whole_t, w_out, m_out, True, ROOT_Q, 2, "step_out"
    )
    keyval_grad = add(*received)
    keyval_grad = dot(keyval_grad, to_whole, ((1,), (1,))).astype(BF16)
    stepped_keyval, new_m_keyval = over_width(
        step_kernel, rate, rows, keyval_grad, w_keyval, m_keyval, True, ROOT_D, 2, "step_keyval"
    )
    (
        partner_query, stepped_keyval, left_in, right_in, across_in, stepped_out, t_across, s_opposite,
        t_right_in, t_left_in, *base
    ) = phase(
        partner_query, stepped_keyval, left_in, right_in, across_in, stepped_out, t_across, s_opposite,
        t_right_in, t_left_in, *base
    )

    partner_keyval = from_partner(stepped_keyval, offset)
    if near_y:
        base[3] = from_partner(base[3], offset)
    t_opposite_in = x_far(add(s_opposite, across_in))
    t_across_in = y_swap(add(t_across, left_in, right_in))
    (avg_out,) = over_width(
        partner_kernel, rate, [partner_rows], partner_mix, stack(*base), stepped_out,
        True, ROOT_Q, 1, "average_out",
    )
    avg_query = average(stepped_query, partner_query)
    attended = add(t_own, t_across_in, t_right_in, t_left_in, t_opposite_in)
    return (
        attended,
        avg_query,
        average(stepped_keyval, partner_keyval),
        avg_out,
        new_m_query,
        new_m_keyval,
        new_m_out,
    )


def per_device(
    tokens, token_ids, cotangent, step_index, norm_gain, q_gain, k_gain,
    w_query, w_keyval, w_out, m_query, m_keyval, m_out,
):
    rate = warm_rate(step_index).reshape(1)
    levels = lax.axis_size("gossip").bit_length() - 1
    branches = [partial(body, 1 << level) for level in range(levels)]
    outs = lax.switch(
        step_index[0] % levels, branches,
        tokens[0], token_ids[0], cotangent[0], rate, norm_gain, q_gain, k_gain,
        w_query[0], w_keyval[0], w_out[0], m_query[0], m_keyval[0], m_out[0],
    )
    return tuple(out[None] for out in outs)


def solution(mesh):
    placed = (
        P("gossip", "tp", None),
        P("gossip", None),
        P("gossip", "tp", None),
        P(),
        P(),
        P(),
        P(),
        P("gossip", None, "tp"),
        P("gossip", "tp", None),
        P("gossip", "tp", None),
        P("gossip", None, "tp"),
        P("gossip", "tp", None),
        P("gossip", "tp", None),
    )
    return jax.shard_map(
        per_device,
        mesh=mesh,
        in_specs=placed,
        out_specs=(
            P("gossip", "tp", None),
            P("gossip", None, "tp"),
            P("gossip", "tp", None),
            P("gossip", "tp", None),
            P("gossip", None, "tp"),
            P("gossip", "tp", None),
            P("gossip", "tp", None),
        ),
        check_vma=False,
    )
```

```python
from functools import partial
import math

import jax
import jax.numpy as jnp
from jax import lax
from jax.experimental import pallas as pl
from jax.experimental.pallas import tpu as pltpu
from jax.sharding import PartitionSpec as P

D = 5120
HD = 128
QH = 32
KVH = 4
S = 1024
ROWS = 64
QUART = 256
VMEM = 36 << 20
VMEM_ALL = 58 << 20
COST = pl.CostEstimate(flops=1, bytes_accessed=1, transcendentals=0)
ROOT_D = math.sqrt(D)
ROOT_Q = math.sqrt(QH * HD)
SCALE = 1.0 / math.sqrt(HD)

norm_eps = 1e-06
rope_base = 1000000.0
end_token = 151643
peak_rate = 0.2
momentum_keep = 0.9

BF16 = jnp.bfloat16
F32 = jnp.float32

NEAR = ((0, 0), (0, 1), (0, 3), (1, 0))
FAR = ((1, 1), (1, 3), (0, 2), (1, 2))


def tp_of(y, x, core):
    return (y % 2) * 8 + (x % 4) * 2 + core % 2


def tp_perm(x, move):
    pairs = []
    for y in range(2):
        for i in range(4):
            for core in range(2):
                pairs.append((tp_of(y, i, core), tp_of(*move(y, i, core))))
    return lax.ppermute(x, "tp", pairs)


def x_plus(v):
    return tp_perm(v, lambda y, i, c: (y, i + 1, c))


def x_minus(v):
    return tp_perm(v, lambda y, i, c: (y, i + 3, c))


def x_far(v):
    return tp_perm(v, lambda y, i, c: (y, i + 2, c))


def y_swap(v):
    return tp_perm(v, lambda y, i, c: (y + 1, i, c))


def core_swap(v):
    return tp_perm(v, lambda y, i, c: (y, i, c + 1))


def from_partner(v, offset):
    count = lax.axis_size("gossip")
    return lax.ppermute(v, "gossip", [(i, (i - offset) % count) for i in range(count)])


def phase(*values):
    return lax.optimization_barrier(values)


def stack(*parts):
    return jnp.concatenate(parts, axis=0)


def blocks_of(quarter):
    return [quarter[i * ROWS : (i + 1) * ROWS] for i in range(4)]


def add(*parts):
    total = parts[0].astype(F32)
    for part in parts[1:]:
        total = total + part.astype(F32)
    return total.astype(BF16)


def kv_users(v, r):
    def move(y, i, c):
        return (i // 2, 2 * (i % 2) + (y + r // 2) % 2, (c + r % 2) % 2)

    return tp_perm(v, move)


def kv_owners(v, r):
    def move(y, i, c):
        return ((i % 2 + r // 2) % 2, y * 2 + i // 2, (c + r % 2) % 2)

    return tp_perm(v, move)


def warm_rate(step_index):
    return peak_rate * (step_index[0] + 1).astype(F32) / 1000.0


def normalize(token_rows, gain):
    floats = token_rows.astype(F32)
    scale = lax.rsqrt(jnp.mean(floats * floats, axis=-1, keepdims=True) + norm_eps)
    return (floats * scale * gain).astype(BF16)


def inverse_freq():
    return rope_base ** (-2.0 * jnp.arange(HD // 2, dtype=F32) / HD)


def dot(a, b, dims):
    return lax.dot_general(a, b, (dims, ((), ())), preferred_element_type=F32)


def spec(shape, index):
    return pl.BlockSpec(shape, index)


def fwd_kernel(
    q_ref, kt_ref, vt_ref, cq_ref, sq_ref, ck_ref, sk_ref, lo_ref, hi_ref, qg_ref, kg_ref,
    mix_ref, p_ref, qr_ref, krt_ref,
):
    half = HD // 2

    @pl.when((pl.program_id(0) == 0) & (pl.program_id(1) == 0))
    def _():
        key = kt_ref[...].astype(F32)
        key = key * lax.rsqrt(jnp.mean(key * key, axis=0, keepdims=True) + norm_eps) * kg_ref[...]
        a, b = key[:half], key[half:]
        cosine, sine = ck_ref[...], sk_ref[...]
        krt_ref[:half] = (a * cosine - b * sine).astype(BF16)
        krt_ref[half:] = (b * cosine + a * sine).astype(BF16)

    query = q_ref[...]
    query = query * lax.rsqrt(jnp.mean(query * query, axis=-1, keepdims=True) + norm_eps)
    query = query * qg_ref[...]
    a, b = query[:, :half], query[:, half:]
    cosine, sine = cq_ref[...], sq_ref[...]
    query_rot = jnp.concatenate([a * cosine - b * sine, b * cosine + a * sine], axis=-1)
    query_rot = query_rot.astype(BF16)
    qr_ref[...] = query_rot
    scores = dot(query_rot, krt_ref[...], ((1,), (0,)))
    place = lax.broadcasted_iota(jnp.int32, scores.shape, 1)
    inside = (place >= lo_ref[...]) & (place <= hi_ref[...])
    weights = jnp.where(inside, jnp.exp(scores * SCALE), 0.0)
    total = jnp.sum(weights, axis=-1, keepdims=True)
    probabilities = (weights * (1.0 / total)).astype(BF16)
    p_ref[0] = probabilities
    mix_ref[...] = dot(probabilities, vt_ref[...], ((1,), (1,))).astype(BF16)


def attention_forward(q, kt, vt, cq, sq, ck, sk, lo, hi, q_gain, k_gain):
    half = HD // 2
    tile = spec((QUART, HD), lambda t, h: (t, h))
    whole = lambda *shape: spec(shape, lambda t, h: (0,) * len(shape))
    column = lambda width: spec((QUART, width), lambda t, h: (t, 0))
    return pl.pallas_call(
        fwd_kernel,
        grid=(4, 2),
        in_specs=[
            tile, whole(HD, S), whole(HD, S), column(half), column(half),
            whole(half, S), whole(half, S), column(1), column(1), whole(1, HD), whole(HD, 1),
        ],
        out_specs=[tile, spec((1, QUART, S), lambda t, h: (h, t, 0)), tile, whole(HD, S)],
        out_shape=[
            jax.ShapeDtypeStruct((S, 2 * HD), BF16),
            jax.ShapeDtypeStruct((2, S, S), BF16),
            jax.ShapeDtypeStruct((S, 2 * HD), BF16),
            jax.ShapeDtypeStruct((HD, S), BF16),
        ],
        compiler_params=pltpu.CompilerParams(vmem_limit_bytes=VMEM),
        cost_estimate=COST,
        name="attention_forward",
    )(q, kt, vt, cq, sq, ck, sk, lo, hi, q_gain.reshape(1, HD), k_gain.reshape(HD, 1))


def bwd_kernel(
    p_ref, do_ref, qr_ref, q_ref, krt_ref, kt_ref, vt_ref, cq_ref, sq_ref, ck_ref, sk_ref,
    qg_ref, kg_ref, dq_ref, dkv_ref, dk_acc, dv_acc,
):
    half = HD // 2
    first = (pl.program_id(0) == 0) & (pl.program_id(1) == 0)
    last = (pl.program_id(0) == 3) & (pl.program_id(1) == 1)

    @pl.when(first)
    def _():
        dk_acc[...] = jnp.zeros_like(dk_acc)
        dv_acc[...] = jnp.zeros_like(dv_acc)

    mix_grad = do_ref[...]
    rounded = p_ref[0]
    prob = rounded.astype(F32)
    dp = dot(mix_grad, vt_ref[...], ((1,), (0,)))
    inner = jnp.sum(prob * dp, axis=-1, keepdims=True)
    ds = (prob * (dp - inner) * SCALE).astype(BF16)
    dq = dot(ds, krt_ref[...], ((1,), (1,))).astype(BF16).astype(F32)
    dv_acc[...] += dot(mix_grad, rounded, ((0,), (0,)))
    dk_acc[...] += dot(qr_ref[...], ds, ((0,), (0,)))
    cosine, sine = cq_ref[...], sq_ref[...]
    da, db = dq[:, :half], dq[:, half:]
    dn = jnp.concatenate([da * cosine + db * sine, db * cosine - da * sine], axis=-1)
    dn = dn * qg_ref[...]
    query = q_ref[...]
    scale = lax.rsqrt(jnp.mean(query * query, axis=-1, keepdims=True) + norm_eps)
    pull = jnp.mean(query * dn, axis=-1, keepdims=True) * scale * scale
    dq_ref[...] = (scale * (dn - query * pull)).astype(BF16)

    @pl.when(last)
    def _():
        dk = dk_acc[...].astype(BF16).astype(F32)
        cosine, sine = ck_ref[...], sk_ref[...]
        da, db = dk[:half], dk[half:]
        dn = jnp.concatenate([da * cosine + db * sine, db * cosine - da * sine], axis=0)
        dn = dn * kg_ref[...]
        key = kt_ref[...].astype(F32)
        scale = lax.rsqrt(jnp.mean(key * key, axis=0, keepdims=True) + norm_eps)
        pull = jnp.mean(key * dn, axis=0, keepdims=True) * scale * scale
        dkv_ref[:HD] = (scale * (dn - key * pull)).astype(BF16)
        dkv_ref[HD:] = dv_acc[...].astype(BF16)


def attention_backward(p, do, qr, q, krt, kt, vt, cq, sq, ck, sk, q_gain, k_gain):
    half = HD // 2
    tile = spec((QUART, HD), lambda t, h: (t, h))
    whole = lambda *shape: spec(shape, lambda t, h: (0,) * len(shape))
    column = lambda width: spec((QUART, width), lambda t, h: (t, 0))
    return pl.pallas_call(
        bwd_kernel,
        grid=(4, 2),
        in_specs=[
            spec((1, QUART, S), lambda t, h: (h, t, 0)), tile, tile, tile,
            whole(HD, S), whole(HD, S), whole(HD, S), column(half), column(half),
            whole(half, S), whole(half, S), whole(1, HD), whole(HD, 1),
        ],
        out_specs=[tile, whole(2 * HD, S)],
        out_shape=[
            jax.ShapeDtypeStruct((S, 2 * HD), BF16),
            jax.ShapeDtypeStruct((2 * HD, S), BF16),
        ],
        scratch_shapes=[pltpu.VMEM((HD, S), F32), pltpu.VMEM((HD, S), F32)],
        compiler_params=pltpu.CompilerParams(vmem_limit_bytes=VMEM_ALL),
        cost_estimate=COST,
        name="attention_backward",
    )(
        p, do, qr, q, krt, kt, vt, cq, sq, ck, sk, q_gain.reshape(1, HD), k_gain.reshape(HD, 1)
    )


def stepped_values(weight, moment, gradient, rate):
    new_moment = momentum_keep * moment.astype(F32) + gradient
    return (weight.astype(F32) - rate * new_moment).astype(BF16), new_moment.astype(BF16)


def product(refs, g_ref, by_rows):
    total, start = None, 0
    for ref in refs:
        span = slice(start, start + ref.shape[0])
        start += ref.shape[0]
        if by_rows:
            term = dot(g_ref[:, span], ref[...], ((1,), (0,)))
        else:
            term = dot(ref[...], g_ref[span], ((0,), (0,)))
        total = term if total is None else total + term
    return total


def step_kernel(count, by_rows, root, rate_ref, *refs):
    g_ref, w_ref, m_ref, stepped_ref, moment_ref = refs[count:]
    gradient = product(refs[:count], g_ref, by_rows) * (1.0 / root)
    stepped_ref[...], moment_ref[...] = stepped_values(
        w_ref[...], m_ref[...], gradient, rate_ref[0]
    )


def partner_kernel(count, by_rows, root, rate_ref, *refs):
    g_ref, base_ref, stepped_ref, avg_ref = refs[count:]
    scaled = product(refs[:count], g_ref, by_rows) * (rate_ref[0] * (1.0 / root))
    partner = base_ref[...].astype(F32) - scaled
    avg_ref[...] = ((stepped_ref[...].astype(F32) + partner) * 0.5).astype(BF16)


def over_width(kernel, rate, parts, factor, first, second, by_rows, root, outs, name, width=512):
    part = [spec((p.shape[0], width), lambda j: (0, j)) for p in parts]
    if by_rows:
        tile = spec((first.shape[0], width), lambda j: (0, j))
    else:
        tile = spec((width, first.shape[1]), lambda j: (j, 0))
    shape = jax.ShapeDtypeStruct(first.shape, BF16)
    return pl.pallas_call(
        partial(kernel, len(parts), by_rows, root),
        grid=(D // width,),
        in_specs=[pl.BlockSpec(memory_space=pltpu.SMEM)] + part
        + [spec(factor.shape, lambda j: (0, 0)), tile, tile],
        out_specs=[tile] * outs,
        out_shape=[shape] * outs,
        compiler_params=pltpu.CompilerParams(vmem_limit_bytes=VMEM_ALL if len(parts) == 1 else VMEM),
        cost_estimate=COST,
        name=name,
    )(rate, *parts, factor, first, second)


def project_kernel(count, *refs):
    parts, (wq_ref, wkv_ref), outs = refs[:count], refs[count : count + 2], refs[count + 2 :]
    if count == 1:
        rows_ref = parts[0]
        q_ref, kv_ref = outs
    else:
        rows_ref, q_ref, kv_ref = outs
        for i, part in enumerate(parts):
            rows_ref[i * ROWS : (i + 1) * ROWS] = part[...]
    q_ref[...] = dot(rows_ref[...], wq_ref[...], ((1,), (0,))) * (1.0 / ROOT_D)
    kv = dot(wkv_ref[...], rows_ref[...], ((1,), (1,))) * (1.0 / ROOT_D)
    kv_ref[...] = kv.astype(BF16)


def project(parts, w_query, w_keyval):
    vmem = pl.BlockSpec(memory_space=pltpu.VMEM)
    shapes = [
        jax.ShapeDtypeStruct((QUART, w_query.shape[1]), F32),
        jax.ShapeDtypeStruct((w_keyval.shape[0], QUART), BF16),
    ]
    if len(parts) > 1:
        shapes = [jax.ShapeDtypeStruct((QUART, D), BF16)] + shapes
    return pl.pallas_call(
        partial(project_kernel, len(parts)),
        in_specs=[vmem] * (len(parts) + 2),
        out_specs=[vmem] * len(shapes),
        out_shape=shapes,
        compiler_params=pltpu.CompilerParams(vmem_limit_bytes=VMEM),
        cost_estimate=COST,
        name="project",
    )(*parts, w_query, w_keyval)


def mix_grad_kernel(order_ref, cot_ref, w_ref, out_ref, acc_ref):
    step = pl.program_id(0)

    @pl.when(step == 0)
    def _():
        acc_ref[...] = jnp.zeros_like(acc_ref)

    acc_ref[...] += dot(cot_ref[...], w_ref[...], ((1,), (1,)))

    @pl.when(step == pl.num_programs(0) - 1)
    def _():
        for i in range(S // ROWS):
            rows = acc_ref[pl.ds(pl.multiple_of(order_ref[i] * ROWS, ROWS), ROWS)]
            out_ref[i * ROWS : (i + 1) * ROWS] = (rows * (1.0 / ROOT_Q)).astype(BF16)


def mix_gradient(order, cot_rows, w_out, width=512):
    cols = w_out.shape[0]
    return pl.pallas_call(
        mix_grad_kernel,
        grid=(D // width,),
        in_specs=[
            pl.BlockSpec(memory_space=pltpu.SMEM),
            spec((S, width), lambda j: (0, j)),
            spec((cols, width), lambda j: (0, j)),
        ],
        out_specs=spec((S, cols), lambda j: (0, 0)),
        out_shape=jax.ShapeDtypeStruct((S, cols), BF16),
        scratch_shapes=[pltpu.VMEM((S, cols), F32)],
        compiler_params=pltpu.CompilerParams(vmem_limit_bytes=VMEM_ALL),
        cost_estimate=COST,
        name="mix_gradient",
    )(order, cot_rows, w_out)


def terms_kernel(mix_ref, w_ref, *outs):
    for i, out in enumerate(outs):
        term = dot(mix_ref[i * QUART : (i + 1) * QUART], w_ref[...], ((1,), (0,)))
        out[...] = (term * (1.0 / ROOT_Q)).astype(BF16)


def output_terms(mix, w_out, width=512):
    cols = w_out.shape[0]
    return pl.pallas_call(
        terms_kernel,
        grid=(D // width,),
        in_specs=[spec((S, cols), lambda j: (0, 0)), spec((cols, width), lambda j: (0, j))],
        out_specs=[spec((QUART, width), lambda j: (0, j))] * 4,
        out_shape=[jax.ShapeDtypeStruct((QUART, D), BF16)] * 4,
        compiler_params=pltpu.CompilerParams(vmem_limit_bytes=VMEM_ALL),
        cost_estimate=COST,
        name="output_terms",
    )(mix, w_out)


def average(stepped, partner):
    return ((stepped.astype(F32) + partner.astype(F32)) * 0.5).astype(BF16)


def body(
    offset,
    tokens, token_ids, cotangent, rate, norm_gain, q_gain, k_gain,
    w_query, w_keyval, w_out, m_query, m_keyval, m_out,
):
    me = lax.axis_index("tp")
    y, x, core = me // 8, (me // 2) % 4, me % 2

    order = []
    for blocks in (NEAR, FAR):
        for other in (0, 1):
            order += [tp_of(y + dy, x + dx, core + other) for dy, dx in blocks]
    order = jnp.stack(order).astype(jnp.int32)
    places = jnp.arange(S, dtype=jnp.int32)
    held = (order[:, None] * ROWS + jnp.arange(ROWS, dtype=jnp.int32)[None]).reshape(S)
    match = held[:, None] == places[None, :]
    closing = (token_ids == end_token).astype(jnp.int32)
    begins = jnp.concatenate([jnp.ones((1,), jnp.int32), closing[:-1]])
    document_start = lax.cummax(jnp.where(begins > 0, places, 0))
    lo = jnp.sum(jnp.where(match, document_start[None, :], 0), axis=1, keepdims=True)
    hi = held[:, None]
    to_whole = match.astype(BF16)
    held_angles = held.astype(F32)[:, None] * inverse_freq()[None]
    whole_angles = inverse_freq()[:, None] * places.astype(F32)[None]
    cq, sq = jnp.cos(held_angles), jnp.sin(held_angles)
    ck, sk = jnp.cos(whole_angles), jnp.sin(whole_angles)

    near_y = offset == 1
    own = normalize(tokens, norm_gain)
    base = (w_out.astype(F32) - rate[0] * (momentum_keep * m_out.astype(F32))).astype(BF16)
    base = blocks_of(base)
    right, left, across, opposite = x_plus(own), x_minus(own), y_swap(own), x_far(own)
    partner_cot = from_partner(cotangent, offset)
    (
        own, right, left, across, opposite, partner_cot, lo, hi, to_whole, cq, sq, ck, sk, cotangent, *base
    ) = phase(
        own, right, left, across, opposite, partner_cot, lo, hi, to_whole, cq, sq, ck, sk, cotangent, *base
    )
    cot_rows = lax.all_gather(cotangent, "tp", axis=0, tiled=True)

    across_right, across_left, across_opposite = x_plus(across), x_minus(across), y_swap(opposite)
    if not near_y:
        base[0] = from_partner(base[0], offset)
    near, query_near, kv_near = project([own, left, right, across], w_query, w_keyval)
    near_other = core_swap(near)
    query_near_other, kv_near_other = project([near_other], w_query, w_keyval)
    (
        across_left, across_right, across_opposite, query_near_other, kv_near_other, *base
    ) = phase(across_left, across_right, across_opposite, query_near_other, kv_near_other, *base)

    partner_rows = lax.all_gather(partner_cot, "tp", axis=0, tiled=True)
    far, query_far, kv_far = project(
        [across_left, across_right, opposite, across_opposite], w_query, w_keyval
    )
    far_other = core_swap(far)
    query_far_other, kv_far_other = project([far_other], w_query, w_keyval)
    rows = (near, near_other, far, far_other)
    kv_held = jnp.concatenate([kv_near, kv_near_other, kv_far, kv_far_other], axis=1)
    kv_own = dot(kv_held, to_whole, ((1,), (0,))).astype(BF16)
    kv_own, *base = phase(kv_own, *base)

    arrived = [kv_users(kv_own, r) for r in range(4)]
    if near_y:
        base[0] = from_partner(base[0], offset)
    else:
        base[1] = from_partner(base[1], offset)
    query = stack(query_near, query_near_other, query_far, query_far_other)
    *arrived, query, base[1], base[2], base[3] = phase(*arrived, query, base[1], base[2], base[3])

    odd_x, odd_core = x % 2 == 1, core == 1

    def in_order(first, second):
        return stack(jnp.where(odd_core, second, first), jnp.where(odd_core, first, second))

    same, other = in_order(arrived[0], arrived[1]), in_order(arrived[2], arrived[3])
    kt, vt = jnp.where(odd_x, other, same), jnp.where(odd_x, same, other)
    mix, prob, query_rot, krt = attention_forward(
        query, kt, vt, cq, sq, ck, sk, lo, hi, q_gain, k_gain
    )
    mix_whole_t = dot(mix, to_whole, ((0,), (0,))).astype(BF16)
    terms = output_terms(mix, w_out)
    cot_rows, mix_whole_t, prob, *base = phase(cot_rows, mix_whole_t, prob, *base)

    partner_mix = from_partner(mix_whole_t, offset)
    if near_y:
        base[1] = from_partner(base[1], offset)
    else:
        base[2], base[3] = from_partner(base[2], offset), from_partner(base[3], offset)
    near_in, far_in = core_swap(terms[1]), core_swap(terms[3])
    mix_grad = mix_gradient(order, cot_rows, w_out)
    query_grad, kv_parts = attention_backward(
        prob, mix_grad, query_rot, query, krt, kt, vt, cq, sq, ck, sk, q_gain, k_gain
    )
    stepped_query, new_m_query = over_width(
        step_kernel, rate, rows, query_grad, w_query, m_query, False, ROOT_D, 2, "step_query"
    )
    kv_parts, stepped_query, mix_whole_t, partner_mix, near_in, far_in, *base = phase(
        kv_parts, stepped_query, mix_whole_t, partner_mix, near_in, far_in, *base
    )

    partner_query = from_partner(stepped_query, offset)
    if near_y:
        base[2] = from_partner(base[2], offset)
    kv_split = kv_parts.reshape(2, 2, ROWS, S)
    received = []
    for r in range(4):
        kind, which = (x + r // 2) % 2, (core + r % 2) % 2
        piece = lax.dynamic_slice(kv_split, (kind, which, 0, 0), (1, 1, ROWS, S))
        received.append(kv_owners(piece.reshape(ROWS, S), r))
    far_sum, near_sum = add(terms[2], far_in), add(terms[0], near_in)
    s_left, s_right, s_opposite, s_across = blocks_of(far_sum)
    t_own, t_left, t_right, t_across = blocks_of(near_sum)
    left_in, right_in, across_in = x_plus(s_left), x_minus(s_right), y_swap(s_across)
    stepped_out, new_m_out = over_width(
        step_kernel, rate, [cot_rows], mix_whole_t, w_out, m_out, True, ROOT_Q, 2, "step_out"
    )
    t_right, t_left, stepped_out = phase(t_right, t_left, stepped_out)
    t_right_in, t_left_in = x_minus(t_right), x_plus(t_left)
    partner_base = base if near_y else [stack(*base)]
    keyval_grad = add(*received)
    keyval_grad = dot(keyval_grad, to_whole, ((1,), (1,))).astype(BF16)
    stepped_keyval, new_m_keyval = over_width(
        step_kernel, rate, rows, keyval_grad, w_keyval, m_keyval, True, ROOT_D, 2, "step_keyval"
    )
    (
        partner_query, stepped_keyval, left_in, right_in, across_in, stepped_out, t_across, s_opposite,
        t_right_in, t_left_in, *partner_base
    ) = phase(
        partner_query, stepped_keyval, left_in, right_in, across_in, stepped_out, t_across, s_opposite,
        t_right_in, t_left_in, *partner_base
    )

    partner_keyval = from_partner(stepped_keyval, offset)
    if near_y:
        partner_base = [stack(*partner_base[:3], from_partner(partner_base[3], offset))]
    t_opposite_in = x_far(add(s_opposite, across_in))
    t_across_in = y_swap(add(t_across, left_in, right_in))
    (avg_out,) = over_width(
        partner_kernel, rate, [partner_rows], partner_mix, partner_base[0], stepped_out,
        True, ROOT_Q, 1, "average_out",
    )
    avg_query = average(stepped_query, partner_query)
    attended = add(t_own, t_across_in, t_right_in, t_left_in, t_opposite_in)
    return (
        attended,
        avg_query,
        average(stepped_keyval, partner_keyval),
        avg_out,
        new_m_query,
        new_m_keyval,
        new_m_out,
    )


def per_device(
    tokens, token_ids, cotangent, step_index, norm_gain, q_gain, k_gain,
    w_query, w_keyval, w_out, m_query, m_keyval, m_out,
):
    rate = warm_rate(step_index).reshape(1)
    levels = lax.axis_size("gossip").bit_length() - 1
    branches = [partial(body, 1 << level) for level in range(levels)]
    outs = lax.switch(
        step_index[0] % levels, branches,
        tokens[0], token_ids[0], cotangent[0], rate, norm_gain, q_gain, k_gain,
        w_query[0], w_keyval[0], w_out[0], m_query[0], m_keyval[0], m_out[0],
    )
    return tuple(out[None] for out in outs)


def solution(mesh):
    placed = (
        P("gossip", "tp", None),
        P("gossip", None),
        P("gossip", "tp", None),
        P(),
        P(),
        P(),
        P(),
        P("gossip", None, "tp"),
        P("gossip", "tp", None),
        P("gossip", "tp", None),
        P("gossip", None, "tp"),
        P("gossip", "tp", None),
        P("gossip", "tp", None),
    )
    return jax.shard_map(
        per_device,
        mesh=mesh,
        in_specs=placed,
        out_specs=(
            P("gossip", "tp", None),
            P("gossip", None, "tp"),
            P("gossip", "tp", None),
            P("gossip", "tp", None),
            P("gossip", None, "tp"),
            P("gossip", "tp", None),
            P("gossip", "tp", None),
        ),
        check_vma=False,
    )
```
